32 devices in a mesh: ep: 32 (over z, y, x, core), tp: 1.
Axes of the slice: x: 2, y: 2, z: 4, core: 2. Of those that a mesh axis runs over, the one named last changes fastest.
Arguments:
- tokens: bfloat16 [1024, 4096], P('ep'), may hold values from -6 to 6
- expert_ids: int32 [1024, 8], P('ep'), may hold values from 0 to 31, all different within a row; in each aligned block of 32 rows (0 to 31, 32 to 63, ...) at most 12 rows name the same one
- gates: float32 [1024, 8], P('ep'), may hold values from 0.05 to 0.5
- w_gate: bfloat16 [32, 768, 4096], P('ep', 'tp'), may hold values from -0.09375 to 0.09375
- w_up: bfloat16 [32, 768, 4096], P('ep', 'tp'), may hold values from -0.09375 to 0.09375
- w_down: bfloat16 [32, 768, 4096], P('ep', 'tp'), may hold values from -0.21875 to 0.21875
- grad_out: bfloat16 [1024, 4096], P('ep'), may hold values from -6 to 6
Outputs:
- layer_out: bfloat16 [1024, 4096], P('ep')
- gate_grads: float32 [1024, 8], P('ep')
- token_grads: bfloat16 [1024, 4096], P('ep')
- grad_gate: bfloat16 [32, 768, 4096], P('ep', 'tp')
- grad_up: bfloat16 [32, 768, 4096], P('ep', 'tp')
- grad_down: bfloat16 [32, 768, 4096], P('ep', 'tp')
The draws below stay inside these ranges and needn't reach their ends.
Inputs may be any that keep to these rules, and one draw needn't show every extreme that they name: `expert_ids`: each row names 8 different experts. Among the rows of one device no expert is named by more than 12 rows, and in some device's rows an expert is named by exactly 12.
All inputs are finite; a program needn't handle non-finite values.
Results may differ from the reference program's by a relative error of at most 0.012.
Values may be sent and summed in bfloat16 or wider, within the bound.
A program may use at most 128 MiB of HBM per device.

```python
import math
import jax
import jax.numpy as jnp
import numpy as np
from jax import lax

D = 4096
TOP = 8
FF = 768
TOK_DEV = 32
EXPERTS = 32
CAP = 12
TOKENS = 1024
N_EP = 32
N_TP = 1


def block_scale(rng, dims, shards, least, high):
    def one(position, blocks):
        steps = jax.random.uniform(jax.random.fold_in(jax.random.fold_in(rng, 6), position), (blocks,), jnp.float32, least / len(shards), high / len(shards))
        return jnp.repeat(jnp.exp(steps), dims[position] // blocks).reshape((-1,) + (1,) * (len(dims) - position - 1))

    factor_of = one(*shards[0])
    for cut in shards[1:]:
        factor_of = factor_of * one(*cut)
    return factor_of


def assign_block(own_key, own, number, rows, number_of, top, limit, slope):
    sequence = jax.random.permutation(own_key, number_of)
    packed, ordinary = shares(number_of, rows * top, limit, slope, True), shares(number_of, rows * top, limit, slope, False)
    places = jnp.arange(number_of)

    def named(sizes, offset_by):
        used = int((sizes > 0).sum())
        fixed = max(1, used // 4)
        shifted = fixed + (places - fixed + offset_by * (used - fixed)) % max(1, number_of - fixed)
        return jnp.zeros((number_of,), jnp.int32).at[sequence[jnp.where(places < fixed, places, shifted)]].set(jnp.asarray(sizes, jnp.int32))

    sizes = jnp.where(number % 4 == 0, named(packed, number // 4), named(ordinary, number - number // 4 - 1))
    mixed = jax.random.permutation(jax.random.fold_in(own, 3), number_of)
    donor, receiver = mixed[0:number_of // 2 * 2:2], mixed[1:number_of // 2 * 2:2]
    slack = jnp.minimum(sizes[donor] - 1, limit - sizes[receiver]) // 2
    slack = jnp.where((donor == sequence[0]) | (receiver == sequence[0]) | (sizes[receiver] == 0), 0, jnp.maximum(slack, 0))
    shifted = jax.random.randint(jax.random.fold_in(own, 4), (number_of // 2,), 0, 1 << 20) % (slack + 1)
    sizes = sizes.at[donor].add(-shifted).at[receiver].add(shifted)
    labels = jnp.searchsorted(jnp.cumsum(sizes), jnp.arange(rows * top), side="right").astype(jnp.int32)
    listing = labels.reshape(top, rows).T
    listing = listing[jax.random.permutation(jax.random.fold_in(own, 1), rows)]
    offset_by = jax.random.randint(jax.random.fold_in(own, 2), (rows, 1), 0, top)
    return jnp.take_along_axis(listing, (jnp.arange(top)[None, :] + offset_by) % top, axis=1)


def shares(count, total, bound, skew, full):
    weights = [(1 << 20) // math.isqrt(standing ** skew) + 1 for standing in range(1, count + 1)]
    largest = bound if full else min(bound, max(-(-total // count), total * weights[0] // sum(weights)))
    least = 1 if total - largest >= count - 1 else 0
    given, spare = [largest] + [least] * (count - 1), total - largest - least * (count - 1)
    while spare > 0:
        movable = [i for i in range(1, count) if given[i] < largest] or [i for i in range(1, count) if given[i] < bound]
        pool, budget = sum([weights[i] for i in movable]), spare
        for i in movable:
            more = min(bound - given[i], max(1, budget * weights[i] // pool), spare)
            given[i] = given[i] + more
            spare = spare - more
    return np.array(given)


def scatter_about(stream_key, extent, deviation, most, cuts=(), held_as=jnp.bfloat16):
    gain = block_scale(stream_key, extent, cuts, -0.22, 0.18) if cuts else 1.0
    values = jax.random.normal(stream_key, extent, jnp.float32) * deviation * gain
    return jnp.minimum(jnp.maximum(values, -most), most).astype(held_as)


def setup_inputs(seed: int = 0) -> dict:
    keys = jax.random.split(jax.random.key(seed), 8)
    tokens = scatter_about(keys[0], (TOKENS, D), 1.0, 6.0, ((0, 32),))
    expert_ids_keys = jax.random.split(jax.random.fold_in(keys[1], 1), TOKENS // TOK_DEV)
    expert_ids_turns = jax.random.permutation(jax.random.fold_in(keys[1], 3), TOKENS // TOK_DEV)
    expert_ids = jax.vmap(lambda own, number: assign_block(jax.random.fold_in(keys[1], 2), own, number, TOK_DEV, EXPERTS, TOP, CAP, 2))(expert_ids_keys, expert_ids_turns).reshape((TOKENS, TOP))
    gates = jnp.clip(jnp.exp(math.log(0.5) - 2.3025851 * jax.random.uniform(keys[2], (TOKENS, TOP), jnp.float32) ** block_scale(keys[2], (TOKENS, TOP), ((0, 32),), -0.2, 0.2)), 0.05, 0.5)
    w_gate = scatter_about(keys[3], (EXPERTS, FF, D), D ** -0.5, 0.09375, ((0, 32),))
    w_up = scatter_about(keys[4], (EXPERTS, FF, D), D ** -0.5, 0.09375, ((0, 32),))
    w_down = scatter_about(keys[5], (EXPERTS, FF, D), FF ** -0.5, 0.21875, ((0, 32),))
    grad_out = scatter_about(keys[6], (TOKENS, D), 1.0, 6.0, ((0, 32),))
    return {"tokens": tokens, "expert_ids": expert_ids, "gates": gates, "w_gate": w_gate, "w_up": w_up, "w_down": w_down, "grad_out": grad_out}


def reference(tokens, expert_ids, gates, w_gate, w_up, w_down, grad_out):
    pairs = TOK_DEV * TOP
    chosen_ids = expert_ids.reshape(N_EP, pairs)
    onehot = (chosen_ids[:, :, None] == jnp.arange(EXPERTS, dtype=jnp.int32)[None, None, :]).astype(jnp.int32)
    before = jnp.cumsum(onehot, axis=1) - onehot
    slot_index = jnp.sum(before * onehot, axis=2).astype(jnp.int32)
    source_dev = jnp.broadcast_to(jnp.arange(N_EP, dtype=jnp.int32)[:, None], (N_EP, pairs))
    token_index = source_dev * TOK_DEV + (jnp.arange(pairs, dtype=jnp.int32) // TOP)[None, :]
    sources = jnp.full((EXPERTS, CAP, N_EP), TOKENS, dtype=jnp.int32)
    sources = sources.at[chosen_ids, slot_index, source_dev].set(token_index.astype(jnp.int32))
    gate_table = jnp.zeros((EXPERTS, CAP, N_EP), jnp.float32)
    gate_table = gate_table.at[chosen_ids, slot_index, source_dev].set(gates.reshape(N_EP, pairs))
    token_pad = jnp.concatenate([tokens, jnp.zeros((1, D), tokens.dtype)], axis=0)
    grad_pad = jnp.concatenate([grad_out, jnp.zeros((1, D), grad_out.dtype)], axis=0)
    row_count = CAP * N_EP
    quarter_width = FF // N_TP

    def quarter_sum(left_mat, right_mat):
        left_q = left_mat.astype(jnp.float32).reshape(row_count, N_TP, quarter_width)
        right_q = right_mat.astype(jnp.float32).reshape(N_TP, quarter_width, D)
        return jnp.einsum("rqf,qfd->qrd", left_q, right_q, precision=lax.Precision.HIGHEST)

    def expert_work(expert):
        rows_from = sources[expert]
        x_rows = token_pad[rows_from].reshape(row_count, D)
        g_rows = (gate_table[expert][:, :, None] * grad_pad[rows_from].astype(jnp.float32)).astype(jnp.bfloat16).reshape(row_count, D)
        gate_mat = w_gate[expert]
        up_mat = w_up[expert]
        down_mat = w_down[expert]
        pre_gate = jnp.dot(x_rows, gate_mat.T, preferred_element_type=jnp.float32)
        pre_up = jnp.dot(x_rows, up_mat.T, preferred_element_type=jnp.float32)
        sigmoid_gate = jax.nn.sigmoid(pre_gate)
        activated = pre_gate * sigmoid_gate
        hidden = (activated * pre_up).astype(jnp.bfloat16)
        parts = lax.optimization_barrier(quarter_sum(hidden, down_mat).astype(jnp.bfloat16))
        out_rows = jnp.sum(parts.astype(jnp.float32), axis=0).astype(jnp.bfloat16)
        grad_hidden = jnp.dot(g_rows, down_mat.T, preferred_element_type=jnp.float32)
        d_up = (grad_hidden * activated).astype(jnp.bfloat16)
        d_gate = (grad_hidden * pre_up * sigmoid_gate * (1.0 + pre_gate * (1.0 - sigmoid_gate))).astype(jnp.bfloat16)
        grad_down_e = jnp.dot(hidden.T, g_rows, preferred_element_type=jnp.float32).astype(jnp.bfloat16)
        grad_gate_e = jnp.dot(d_gate.T, x_rows, preferred_element_type=jnp.float32).astype(jnp.bfloat16)
        grad_up_e = jnp.dot(d_up.T, x_rows, preferred_element_type=jnp.float32).astype(jnp.bfloat16)
        back_parts = quarter_sum(d_gate, gate_mat) + quarter_sum(d_up, up_mat)
        back_parts = lax.optimization_barrier(back_parts.astype(jnp.bfloat16))
        back_rows = jnp.sum(back_parts.astype(jnp.float32), axis=0).astype(jnp.bfloat16)
        return (out_rows.reshape(CAP, N_EP, D), back_rows.reshape(CAP, N_EP, D), grad_gate_e, grad_up_e, grad_down_e)

    out_all, back_all, grad_gate, grad_up, grad_down = lax.map(expert_work, jnp.arange(EXPERTS, dtype=jnp.int32))
    picked_out = out_all[chosen_ids, slot_index, source_dev].reshape(TOKENS, TOP, D).astype(jnp.float32)
    picked_back = back_all[chosen_ids, slot_index, source_dev].reshape(TOKENS, TOP, D).astype(jnp.float32)
    layer_out = jnp.einsum("tk,tkd->td", gates, picked_out, precision=lax.Precision.HIGHEST).astype(jnp.bfloat16)
    gate_grads = jnp.einsum("tkd,td->tk", picked_out, grad_out.astype(jnp.float32), precision=lax.Precision.HIGHEST)
    token_grads = jnp.sum(picked_back, axis=1).astype(jnp.bfloat16)
    return (layer_out, gate_grads, token_grads, grad_gate, grad_up, grad_down)
```

```python
import jax
import jax.numpy as jnp
from jax import lax
from jax.sharding import PartitionSpec as P


def on_device(tokens, expert_ids, gates, w_gate, w_up, w_down, grad_out):
    token_count, model_width = tokens.shape
    chosen = expert_ids.shape[1]
    ep_size = lax.axis_size("ep")
    tp_size = lax.axis_size("tp")
    capacity = tp_size * max(
        1, min(token_count, 3 * token_count * chosen // (2 * ep_size)) // tp_size
    )
    me = lax.axis_index("ep")
    group = 8
    groups = ep_size // group
    all_tokens = ep_size * token_count
    routing = jnp.concatenate([expert_ids.astype(jnp.float32), gates], axis=1)
    all_routing = lax.all_gather(routing, "ep", axis=0, tiled=True)
    x_all = lax.all_gather(tokens, "ep", axis=0, tiled=True)
    d_all = lax.all_gather(grad_out, "ep", axis=0, tiled=True)
    all_ids = all_routing[:, :chosen]
    all_gates = all_routing[:, chosen:]
    hit = all_ids == me.astype(jnp.float32)
    token_gate = jnp.sum(jnp.where(hit, all_gates, 0.0), axis=1)
    token_hit = jnp.any(hit, axis=1).reshape(ep_size, token_count)
    counted = token_hit.astype(jnp.int32)
    slot = jnp.cumsum(counted, axis=1) - counted
    place = jnp.where(token_hit, slot, -1).reshape(groups, group, token_count)
    same = jnp.eye(group, dtype=jnp.bool_)[None, :, None, :, None]
    pick = (
        same
        & (
            place[:, None, None, :, :]
            == jnp.arange(capacity, dtype=jnp.int32)[None, None, :, None, None]
        )
    ).reshape(groups, group * capacity, group * token_count)
    picker = pick.astype(jnp.bfloat16)
    row_gate = jnp.sum(
        jnp.where(pick, token_gate.reshape(groups, 1, group * token_count), 0.0), axis=2
    ).reshape(-1, 1)
    rows = ep_size * capacity

    def take(full):
        return (
            lax.dot_general(
                picker,
                full.reshape(groups, group * token_count, model_width),
                (((2,), (1,)), ((0,), (0,))),
                preferred_element_type=jnp.float32,
            )
            .astype(jnp.bfloat16)
            .reshape(rows, model_width)
        )

    def put(part):
        return (
            lax.dot_general(
                picker,
                part.reshape(groups, group * capacity, model_width),
                (((1,), (1,)), ((0,), (0,))),
                preferred_element_type=jnp.float32,
            )
            .astype(jnp.bfloat16)
            .reshape(all_tokens, model_width)
        )

    gate_mat = w_gate[0]
    up_mat = w_up[0]
    down_mat = w_down[0]
    contract = (((1,), (1,)), ((), ()))
    over_rows = (((0,), (0,)), ((), ()))
    plain = (((1,), (0,)), ((), ()))
    f32 = jnp.float32
    x_rows = take(x_all)
    pre_gate = lax.dot_general(x_rows, gate_mat, contract, preferred_element_type=f32)
    pre_up = lax.dot_general(x_rows, up_mat, contract, preferred_element_type=f32)
    sig = jax.nn.sigmoid(pre_gate)
    activated = pre_gate * sig
    hidden = activated * pre_up
    hidden_gated = (hidden * row_gate).astype(jnp.bfloat16)
    out_rows = lax.dot_general(hidden_gated, down_mat, plain, preferred_element_type=f32)
    layer_part = put(out_rows.astype(jnp.bfloat16))
    layer_out = lax.psum_scatter(layer_part, "ep", scatter_dimension=0, tiled=True)
    d_rows = take(d_all)
    raw_hidden = lax.dot_general(d_rows, down_mat, contract, preferred_element_type=f32)
    row_dot = jnp.sum(raw_hidden * hidden, axis=1, keepdims=True)
    grad_hidden = raw_hidden * row_gate
    d_up = (grad_hidden * activated).astype(jnp.bfloat16)
    d_gate = (grad_hidden * pre_up * sig * (1.0 + pre_gate * (1.0 - sig))).astype(jnp.bfloat16)
    back_rows = lax.dot_general(d_gate, gate_mat, plain, preferred_element_type=f32)
    back_rows = back_rows + lax.dot_general(d_up, up_mat, plain, preferred_element_type=f32)
    token_part = put(back_rows.astype(jnp.bfloat16))
    token_grads = lax.psum_scatter(token_part, "ep", scatter_dimension=0, tiled=True)
    token_dot = jnp.sum(
        jnp.where(pick, row_dot.reshape(groups, group * capacity, 1), 0.0), axis=1
    ).reshape(ep_size, token_count)
    expert_dot = lax.all_to_all(token_dot, "ep", split_axis=0, concat_axis=0, tiled=True)
    if tp_size > 1:
        layer_out = lax.psum(layer_out, "tp")
        token_grads = lax.psum(token_grads, "tp")
        expert_dot = lax.psum(expert_dot, "tp")
    chosen_here = expert_ids[:, :, None] == jnp.arange(ep_size, dtype=jnp.int32)[None, None, :]
    gate_grads = jnp.sum(jnp.where(chosen_here, expert_dot.T[:, None, :], 0.0), axis=2)
    down_grad = lax.dot_general(hidden_gated, d_rows, over_rows, preferred_element_type=f32)
    gate_weight_grad = lax.dot_general(d_gate, x_rows, over_rows, preferred_element_type=f32)
    up_weight_grad = lax.dot_general(d_up, x_rows, over_rows, preferred_element_type=f32)
    return (
        layer_out,
        gate_grads,
        token_grads,
        gate_weight_grad.astype(jnp.bfloat16)[None],
        up_weight_grad.astype(jnp.bfloat16)[None],
        down_grad.astype(jnp.bfloat16)[None],
    )


def solution(mesh):
    placed = (
        P("ep", None),
        P("ep", None),
        P("ep", None),
        P("ep", "tp", None),
        P("ep", "tp", None),
        P("ep", "tp", None),
        P("ep", None),
    )
    return jax.shard_map(
        on_device,
        mesh=mesh,
        in_specs=placed,
        out_specs=(
            P("ep", None),
            P("ep", None),
            P("ep", None),
            P("ep", "tp", None),
            P("ep", "tp", None),
            P("ep", "tp", None),
        ),
        check_vma=False,
    )
```

```python
import functools
import jax
import jax.numpy as jnp
from jax import lax
from jax.experimental import pallas as pl
from jax.experimental.pallas import tpu as pltpu
from jax.sharding import PartitionSpec as P

MESH = pl.DeviceIdType.MESH
Z = 4


def places():
    me = lax.axis_index("ep")
    core, x, y, z = me % 2, (me // 2) % 2, (me // 4) % 2, me // 8

    def dev(back, dy, dx, dc):
        yy = 1 - y if dy else y
        xx = 1 - x if dx else x
        cc = 1 - core if dc else core
        return ((z + back) % Z) * 8 + yy * 4 + xx * 2 + cc

    return me, dev


def greet(dev):
    barrier = pltpu.get_barrier_semaphore()
    tp = lax.axis_index("tp")
    peers = [dev(0, 0, 1, 0), dev(0, 1, 0, 0), dev(0, 0, 0, 1)] + [
        dev(j, 0, 0, 0) for j in range(1, Z)
    ]
    for peer in peers:
        pl.semaphore_signal(barrier, inc=1, device_id=(peer, tp), device_id_type=MESH)
    pl.semaphore_wait(barrier, len(peers))
    return tp


def gather_kernel(rows, a_ref, r_ref, out_ref, rout_ref, send, recv, rsend, rrecv, local):
    me, dev = places()
    tp = greet(dev)

    def at(ref, origin):
        return ref.at[pl.ds(pl.multiple_of(origin * rows, rows), rows)]

    def copies(k, origin, target):
        return (
            pltpu.make_async_remote_copy(
                src_ref=at(out_ref, origin), dst_ref=at(out_ref, origin),
                send_sem=send.at[k], recv_sem=recv.at[k],
                device_id=(target, tp), device_id_type=MESH,
            ),
            pltpu.make_async_remote_copy(
                src_ref=at(rout_ref, origin), dst_ref=at(rout_ref, origin),
                send_sem=rsend.at[k], recv_sem=rrecv.at[k],
                device_id=(target, tp), device_id_type=MESH,
            ),
        )

    started = []

    def push(k, origin, target):
        for copy in copies(k, origin, target):
            copy.start()
            started.append(copy)

    def arrived(k, origin):
        for copy in copies(k, origin, dev(0, 0, 0, 1)):
            copy.wait_recv()

    xn, yn, cn = dev(0, 0, 1, 0), dev(0, 1, 0, 0), dev(0, 0, 0, 1)
    first = pltpu.make_async_copy(a_ref, at(out_ref, me), local.at[0])
    second = pltpu.make_async_copy(r_ref, at(rout_ref, me), local.at[1])
    first.start()
    second.start()
    first.wait()
    second.wait()
    push(3, me, xn)
    push(7, me, yn)
    for j in range(1, Z):
        push(j - 1, me, dev(j, 0, 0, 0))
    push(15, me, cn)
    for step in range(1, Z + 2):
        j = step
        if j < Z:
            own = dev(Z - j, 0, 0, 0)
            arrived(j - 1, own)
            push(3 + j, own, xn)
            push(7 + j, own, yn)
            push(15 + 4 * j, own, cn)
        j = step - 1
        if 0 <= j < Z:
            from_x, from_y = dev(Z - j, 0, 1, 0), dev(Z - j, 1, 0, 0)
            arrived(3 + j, from_x)
            if j % 2 == 0:
                push(11 + j, from_x, yn)
            push(15 + 4 * j + 1, from_x, cn)
            arrived(7 + j, from_y)
            if j % 2 == 1:
                push(11 + j, from_y, xn)
            push(15 + 4 * j + 2, from_y, cn)
        j = step - 2
        if 0 <= j < Z:
            diagonal = dev(Z - j, 1, 1, 0)
            arrived(11 + j, diagonal)
            push(15 + 4 * j + 3, diagonal, cn)
    for j in range(Z):
        for d in range(4):
            arrived(15 + 4 * j + d, dev(Z - j, d // 2, d % 2, 1))
    for copy in started:
        copy.wait_send()


def gather(rows_in, routing, ep_size):
    rows, width = rows_in.shape
    n = 2 * Z * 4 - 1
    return pl.pallas_call(
        functools.partial(gather_kernel, rows),
        out_shape=(
            jax.ShapeDtypeStruct((ep_size * rows, width), rows_in.dtype),
            jax.ShapeDtypeStruct((ep_size * rows, routing.shape[1]), routing.dtype),
        ),
        in_specs=[pl.BlockSpec(memory_space=pl.ANY)] * 2,
        out_specs=[pl.BlockSpec(memory_space=pl.ANY)] * 2,
        scratch_shapes=[pltpu.SemaphoreType.DMA((n,))] * 4 + [pltpu.SemaphoreType.DMA((2,))],
        compiler_params=pltpu.CompilerParams(collective_id=0, has_side_effects=True),
    )(rows_in, routing)


def scatter_kernel(rows, p_ref, o_ref, cbuf, dbuf, xbuf, ybuf, zbuf, send, recv):
    me, dev = places()
    tp = greet(dev)
    width = p_ref.shape[1]
    part = 512

    def copy_of(k, src, dst, target):
        return pltpu.make_async_remote_copy(
            src_ref=src, dst_ref=dst, send_sem=send.at[k], recv_sem=recv.at[k],
            device_id=(target, tp), device_id_type=MESH,
        )

    started = []

    def push(k, src, dst, target):
        copy = copy_of(k, src, dst, target)
        copy.start()
        started.append(copy)

    def arrived(k, dst):
        copy_of(k, dst, dst, dev(0, 0, 0, 1)).wait_recv()

    def total(dst, *refs):
        def body(c, carry):
            cols = pl.ds(pl.multiple_of(c * part, part), part)
            acc = refs[0][:, cols].astype(jnp.float32)
            for ref in refs[1:]:
                acc = acc + ref[:, cols].astype(jnp.float32)
            dst[:, cols] = acc.astype(dst.dtype)
            return carry

        lax.fori_loop(0, width // part, body, 0)

    def mine(origin):
        return p_ref.at[pl.ds(pl.multiple_of(origin * rows, rows), rows)]

    xn, yn, cn = dev(0, 0, 1, 0), dev(0, 1, 0, 0), dev(0, 0, 0, 1)
    order = [1, 2, 3, 0]
    for j in order:
        for d in (3, 1, 2, 0):
            push(15 + 4 * j + d, mine(dev(j, d // 2, d % 2, 1)), cbuf.at[4 * j + d], cn)

    def meet(j, d):
        spot = cbuf.at[4 * j + d]
        arrived(15 + 4 * j + d, spot)
        total(spot, spot, mine(dev(j, d // 2, d % 2, 0)))
        return spot

    for step in range(Z + 2):
        if step < Z:
            j = order[step]
            push(11 + j, meet(j, 3), dbuf.at[j], yn if j % 2 == 0 else xn)
            x_part, y_part = meet(j, 1), meet(j, 2)
            if j % 2 == 0:
                push(7 + j, y_part, ybuf.at[j], yn)
            else:
                push(3 + j, x_part, xbuf.at[j], xn)
            meet(j, 0)
        if 1 <= step <= Z:
            j = order[step - 1]
            arrived(11 + j, dbuf.at[j])
            if j % 2 == 0:
                spot = cbuf.at[4 * j + 1]
                total(spot, spot, dbuf.at[j])
                push(3 + j, spot, xbuf.at[j], xn)
            else:
                spot = cbuf.at[4 * j + 2]
                total(spot, spot, dbuf.at[j])
                push(7 + j, spot, ybuf.at[j], yn)
        if step >= 2:
            j = order[step - 2]
            arrived(3 + j, xbuf.at[j])
            arrived(7 + j, ybuf.at[j])
            spot = cbuf.at[4 * j]
            if j > 0:
                total(spot, spot, xbuf.at[j], ybuf.at[j])
                push(j - 1, spot, zbuf.at[j - 1], dev(j, 0, 0, 0))
    for j in range(1, Z):
        arrived(j - 1, zbuf.at[j - 1])
    total(o_ref, cbuf.at[0], xbuf.at[0], ybuf.at[0], zbuf.at[0], zbuf.at[1], zbuf.at[2])
    for copy in started:
        copy.wait_send()


def scatter(partial, rows):
    width = partial.shape[1]
    n = 2 * Z * 4 - 1
    return pl.pallas_call(
        functools.partial(scatter_kernel, rows),
        out_shape=jax.ShapeDtypeStruct((rows, width), partial.dtype),
        in_specs=[pl.BlockSpec(memory_space=pltpu.VMEM)],
        out_specs=pl.BlockSpec(memory_space=pltpu.VMEM),
        scratch_shapes=[
            pltpu.VMEM((4 * Z, rows, width), partial.dtype),
            pltpu.VMEM((Z, rows, width), partial.dtype),
            pltpu.VMEM((Z, rows, width), partial.dtype),
            pltpu.VMEM((Z, rows, width), partial.dtype),
            pltpu.VMEM((Z - 1, rows, width), partial.dtype),
            pltpu.SemaphoreType.DMA((n,)),
            pltpu.SemaphoreType.DMA((n,)),
        ],
        compiler_params=pltpu.CompilerParams(
            collective_id=1, has_side_effects=True, vmem_limit_bytes=48 * 1024 * 1024
        ),
    )(partial)


def on_device(tokens, expert_ids, gates, w_gate, w_up, w_down, grad_out):
    token_count, model_width = tokens.shape
    chosen = expert_ids.shape[1]
    ep_size = lax.axis_size("ep")
    tp_size = lax.axis_size("tp")
    capacity = tp_size * max(
        1, min(token_count, 3 * token_count * chosen // (2 * ep_size)) // tp_size
    )
    me = lax.axis_index("ep")
    group = 8
    groups = ep_size // group
    all_tokens = ep_size * token_count
    routing = jnp.concatenate([expert_ids.astype(jnp.float32), gates], axis=1)
    both = jnp.concatenate([tokens, grad_out], axis=1)
    own_kernels = ep_size == 8 * Z and tp_size == 1
    if own_kernels:
        routing = jnp.pad(routing, ((0, 0), (0, 128 - 2 * chosen)))
        both_all, all_routing = gather(both, routing, ep_size)
    else:
        all_routing = lax.all_gather(routing, "ep", axis=0, tiled=True)
        both_all = lax.all_gather(both, "ep", axis=0, tiled=True)
    all_ids = all_routing[:, :chosen]
    all_gates = all_routing[:, chosen : 2 * chosen]
    hit = all_ids == me.astype(jnp.float32)
    token_gate = jnp.sum(jnp.where(hit, all_gates, 0.0), axis=1)
    token_hit = jnp.any(hit, axis=1).reshape(ep_size, token_count)
    counted = token_hit.astype(jnp.int32)
    slot = jnp.cumsum(counted, axis=1) - counted
    place = jnp.where(token_hit, slot, -1).reshape(groups, group, token_count)
    same = jnp.eye(group, dtype=jnp.bool_)[None, :, None, :, None]
    pick = (
        same
        & (
            place[:, None, None, :, :]
            == jnp.arange(capacity, dtype=jnp.int32)[None, None, :, None, None]
        )
    ).reshape(groups, group * capacity, group * token_count)
    picker = pick.astype(jnp.bfloat16)
    row_gate = jnp.sum(
        jnp.where(pick, token_gate.reshape(groups, 1, group * token_count), 0.0), axis=2
    ).reshape(-1, 1)
    rows = ep_size * capacity

    def take(full):
        return (
            lax.dot_general(
                picker,
                full.reshape(groups, group * token_count, 2 * model_width),
                (((2,), (1,)), ((0,), (0,))),
                preferred_element_type=jnp.float32,
            )
            .astype(jnp.bfloat16)
            .reshape(rows, 2 * model_width)
        )

    def put(part):
        return (
            lax.dot_general(
                picker,
                part.reshape(groups, group * capacity, 2 * model_width),
                (((1,), (1,)), ((0,), (0,))),
                preferred_element_type=jnp.float32,
            )
            .astype(jnp.bfloat16)
            .reshape(all_tokens, 2 * model_width)
        )

    gate_mat = w_gate[0]
    up_mat = w_up[0]
    down_mat = w_down[0]
    contract = (((1,), (1,)), ((), ()))
    over_rows = (((0,), (0,)), ((), ()))
    plain = (((1,), (0,)), ((), ()))
    f32 = jnp.float32
    both_rows = take(both_all)
    x_rows, d_rows = both_rows[:, :model_width], both_rows[:, model_width:]
    pre_gate = lax.dot_general(x_rows, gate_mat, contract, preferred_element_type=f32)
    pre_up = lax.dot_general(x_rows, up_mat, contract, preferred_element_type=f32)
    sig = jax.nn.sigmoid(pre_gate)
    activated = pre_gate * sig
    hidden = activated * pre_up
    hidden_gated = (hidden * row_gate).astype(jnp.bfloat16)
    out_rows = lax.dot_general(hidden_gated, down_mat, plain, preferred_element_type=f32)
    raw_hidden = lax.dot_general(d_rows, down_mat, contract, preferred_element_type=f32)
    row_dot = jnp.sum(raw_hidden * hidden, axis=1, keepdims=True)
    grad_hidden = raw_hidden * row_gate
    d_up = (grad_hidden * activated).astype(jnp.bfloat16)
    d_gate = (grad_hidden * pre_up * sig * (1.0 + pre_gate * (1.0 - sig))).astype(jnp.bfloat16)
    back_rows = lax.dot_general(d_gate, gate_mat, plain, preferred_element_type=f32)
    back_rows = back_rows + lax.dot_general(d_up, up_mat, plain, preferred_element_type=f32)
    result_rows = jnp.concatenate(
        [out_rows.astype(jnp.bfloat16), back_rows.astype(jnp.bfloat16)], axis=1
    )
    partial = put(result_rows)
    if own_kernels:
        summed = scatter(partial, token_count)
    else:
        summed = lax.psum_scatter(partial, "ep", scatter_dimension=0, tiled=True)
    token_dot = jnp.sum(
        jnp.where(pick, row_dot.reshape(groups, group * capacity, 1), 0.0), axis=1
    ).reshape(ep_size, token_count)
    expert_dot = lax.all_to_all(token_dot, "ep", split_axis=0, concat_axis=0, tiled=True)
    if tp_size > 1:
        summed = lax.psum(summed, "tp")
        expert_dot = lax.psum(expert_dot, "tp")
    chosen_here = expert_ids[:, :, None] == jnp.arange(ep_size, dtype=jnp.int32)[None, None, :]
    gate_grads = jnp.sum(jnp.where(chosen_here, expert_dot.T[:, None, :], 0.0), axis=2)
    down_grad = lax.dot_general(hidden_gated, d_rows, over_rows, preferred_element_type=f32)
    gate_weight_grad = lax.dot_general(d_gate, x_rows, over_rows, preferred_element_type=f32)
    up_weight_grad = lax.dot_general(d_up, x_rows, over_rows, preferred_element_type=f32)
    return (
        summed[:, :model_width],
        gate_grads,
        summed[:, model_width:],
        gate_weight_grad.astype(jnp.bfloat16)[None],
        up_weight_grad.astype(jnp.bfloat16)[None],
        down_grad.astype(jnp.bfloat16)[None],
    )


def solution(mesh):
    placed = (
        P("ep", None),
        P("ep", None),
        P("ep", None),
        P("ep", "tp", None),
        P("ep", "tp", None),
        P("ep", "tp", None),
        P("ep", None),
    )
    return jax.shard_map(
        on_device,
        mesh=mesh,
        in_specs=placed,
        out_specs=(
            P("ep", None),
            P("ep", None),
            P("ep", None),
            P("ep", "tp", None),
            P("ep", "tp", None),
            P("ep", "tp", None),
        ),
        check_vma=False,
    )
```

```python
import functools
import jax
import jax.numpy as jnp
from jax import lax
from jax.experimental import pallas as pl
from jax.experimental.pallas import tpu as pltpu
from jax.sharding import PartitionSpec as P

MESH = pl.DeviceIdType.MESH
Z = 4


def places():
    me = lax.axis_index("ep")
    core, x, y, z = me % 2, (me // 2) % 2, (me // 4) % 2, me // 8

    def dev(back, dy, dx, dc):
        yy = 1 - y if dy else y
        xx = 1 - x if dx else x
        cc = 1 - core if dc else core
        return ((z + back) % Z) * 8 + yy * 4 + xx * 2 + cc

    return me, dev


def greet(dev):
    barrier = pltpu.get_barrier_semaphore()
    tp = lax.axis_index("tp")
    peers = [dev(0, 0, 1, 0), dev(0, 1, 0, 0), dev(0, 0, 0, 1)] + [
        dev(j, 0, 0, 0) for j in range(1, Z)
    ]
    for peer in peers:
        pl.semaphore_signal(barrier, inc=1, device_id=(peer, tp), device_id_type=MESH)
    pl.semaphore_wait(barrier, len(peers))
    return tp


def gather_kernel(rows, a_ref, r_ref, out_ref, rout_ref, send, recv, rsend, rrecv, local):
    me, dev = places()
    tp = greet(dev)

    def at(ref, origin):
        return ref.at[pl.ds(pl.multiple_of(origin * rows, rows), rows)]

    def copies(k, origin, target):
        return (
            pltpu.make_async_remote_copy(
                src_ref=at(out_ref, origin), dst_ref=at(out_ref, origin),
                send_sem=send.at[k], recv_sem=recv.at[k],
                device_id=(target, tp), device_id_type=MESH,
            ),
            pltpu.make_async_remote_copy(
                src_ref=at(rout_ref, origin), dst_ref=at(rout_ref, origin),
                send_sem=rsend.at[k], recv_sem=rrecv.at[k],
                device_id=(target, tp), device_id_type=MESH,
            ),
        )

    started = []

    def push(k, origin, target):
        for copy in copies(k, origin, target):
            copy.start()
            started.append(copy)

    def arrived(k, origin):
        for copy in copies(k, origin, dev(0, 0, 0, 1)):
            copy.wait_recv()

    xn, yn, cn = dev(0, 0, 1, 0), dev(0, 1, 0, 0), dev(0, 0, 0, 1)
    first = pltpu.make_async_copy(a_ref, at(out_ref, me), local.at[0])
    second = pltpu.make_async_copy(r_ref, at(rout_ref, me), local.at[1])
    first.start()
    second.start()
    first.wait()
    second.wait()
    for j in range(1, Z):
        push(j - 1, me, dev(j, 0, 0, 0))
    push(3, me, xn)
    push(7, me, yn)
    push(15, me, cn)
    for step in range(1, Z + 2):
        j = step
        if j < Z:
            own = dev(Z - j, 0, 0, 0)
            arrived(j - 1, own)
            push(3 + j, own, xn)
            push(7 + j, own, yn)
            push(15 + 4 * j, own, cn)
        j = step - 1
        if 0 <= j < Z:
            from_x, from_y = dev(Z - j, 0, 1, 0), dev(Z - j, 1, 0, 0)
            arrived(3 + j, from_x)
            if j % 2 == 0:
                push(11 + j, from_x, yn)
            push(15 + 4 * j + 1, from_x, cn)
            arrived(7 + j, from_y)
            if j % 2 == 1:
                push(11 + j, from_y, xn)
            push(15 + 4 * j + 2, from_y, cn)
        j = step - 2
        if 0 <= j < Z:
            diagonal = dev(Z - j, 1, 1, 0)
            arrived(11 + j, diagonal)
            push(15 + 4 * j + 3, diagonal, cn)
    for j in range(Z):
        for d in range(4):
            arrived(15 + 4 * j + d, dev(Z - j, d // 2, d % 2, 1))
    for copy in started:
        copy.wait_send()


def gather(rows_in, routing, ep_size):
    rows, width = rows_in.shape
    n = 2 * Z * 4 - 1
    return pl.pallas_call(
        functools.partial(gather_kernel, rows),
        out_shape=(
            jax.ShapeDtypeStruct((ep_size * rows, width), rows_in.dtype),
            jax.ShapeDtypeStruct((ep_size * rows, routing.shape[1]), routing.dtype),
        ),
        in_specs=[pl.BlockSpec(memory_space=pl.ANY)] * 2,
        out_specs=[pl.BlockSpec(memory_space=pl.ANY)] * 2,
        scratch_shapes=[pltpu.SemaphoreType.DMA((n,))] * 4 + [pltpu.SemaphoreType.DMA((2,))],
        compiler_params=pltpu.CompilerParams(collective_id=0, has_side_effects=True),
    )(rows_in, routing)


def scatter_kernel(rows, p_ref, o_ref, pbuf, cbuf, dbuf, xbuf, ybuf, zbuf, send, recv, local):
    me, dev = places()
    tp = greet(dev)
    width = p_ref.shape[1]
    part = 640 if width % 640 == 0 else 128

    def copy_of(k, src, dst, target):
        return pltpu.make_async_remote_copy(
            src_ref=src, dst_ref=dst, send_sem=send.at[k], recv_sem=recv.at[k],
            device_id=(target, tp), device_id_type=MESH,
        )

    started = []

    def push(k, src, dst, target):
        copy = copy_of(k, src, dst, target)
        copy.start()
        started.append(copy)

    def arrived(k, dst):
        copy_of(k, dst, dst, dev(0, 0, 0, 1)).wait_recv()

    def total(dst, *refs):
        def body(c, carry):
            cols = pl.ds(pl.multiple_of(c * part, part), part)
            acc = refs[0][:, cols].astype(jnp.float32)
            for ref in refs[1:]:
                acc = acc + ref[:, cols].astype(jnp.float32)
            dst[:, cols] = acc.astype(dst.dtype)
            return carry

        lax.fori_loop(0, width // part, body, 0)

    def mine(origin):
        return p_ref.at[pl.ds(pl.multiple_of(origin * rows, rows), rows)]

    xn, yn, cn = dev(0, 0, 1, 0), dev(0, 1, 0, 0), dev(0, 0, 0, 1)
    order = [1, 2, 3, 0]
    for j in order:
        for d in (3, 1, 2, 0):
            push(15 + 4 * j + d, mine(dev(j, d // 2, d % 2, 1)), cbuf.at[4 * j + d], cn)

    def fetch(j, d):
        return pltpu.make_async_copy(
            mine(dev(j, d // 2, d % 2, 0)), pbuf.at[4 * j + d], local.at[4 * j + d]
        )

    for j in order:
        for d in (3, 1, 2, 0):
            fetch(j, d).start()

    def meet(j, d):
        spot = cbuf.at[4 * j + d]
        fetch(j, d).wait()
        arrived(15 + 4 * j + d, spot)
        total(spot, spot, pbuf.at[4 * j + d])
        return spot

    for step in range(Z + 2):
        if step < Z:
            j = order[step]
            push(11 + j, meet(j, 3), dbuf.at[j], yn if j % 2 == 0 else xn)
            x_part, y_part = meet(j, 1), meet(j, 2)
            if j % 2 == 0:
                push(7 + j, y_part, ybuf.at[j], yn)
            else:
                push(3 + j, x_part, xbuf.at[j], xn)
            meet(j, 0)
        if 1 <= step <= Z:
            j = order[step - 1]
            arrived(11 + j, dbuf.at[j])
            if j % 2 == 0:
                spot = cbuf.at[4 * j + 1]
                total(spot, spot, dbuf.at[j])
                push(3 + j, spot, xbuf.at[j], xn)
            else:
                spot = cbuf.at[4 * j + 2]
                total(spot, spot, dbuf.at[j])
                push(7 + j, spot, ybuf.at[j], yn)
        if step >= 2:
            j = order[step - 2]
            arrived(3 + j, xbuf.at[j])
            arrived(7 + j, ybuf.at[j])
            spot = cbuf.at[4 * j]
            if j > 0:
                total(spot, spot, xbuf.at[j], ybuf.at[j])
                push(j - 1, spot, zbuf.at[j - 1], dev(j, 0, 0, 0))
    for j in range(1, Z):
        arrived(j - 1, zbuf.at[j - 1])
    total(o_ref, cbuf.at[0], xbuf.at[0], ybuf.at[0], zbuf.at[0], zbuf.at[1], zbuf.at[2])
    for copy in started:
        copy.wait_send()


def scatter(partial, rows):
    width = partial.shape[1]
    n = 2 * Z * 4 - 1
    return pl.pallas_call(
        functools.partial(scatter_kernel, rows),
        out_shape=jax.ShapeDtypeStruct((rows, width), partial.dtype),
        in_specs=[pl.BlockSpec(memory_space=pl.ANY)],
        out_specs=pl.BlockSpec(memory_space=pltpu.VMEM),
        scratch_shapes=[
            pltpu.VMEM((4 * Z, rows, width), partial.dtype),
            pltpu.VMEM((4 * Z, rows, width), partial.dtype),
            pltpu.VMEM((Z, rows, width), partial.dtype),
            pltpu.VMEM((Z, rows, width), partial.dtype),
            pltpu.VMEM((Z, rows, width), partial.dtype),
            pltpu.VMEM((Z - 1, rows, width), partial.dtype),
            pltpu.SemaphoreType.DMA((n,)),
            pltpu.SemaphoreType.DMA((n,)),
            pltpu.SemaphoreType.DMA((4 * Z,)),
        ],
        compiler_params=pltpu.CompilerParams(
            collective_id=1, has_side_effects=True, vmem_limit_bytes=48 * 1024 * 1024
        ),
    )(partial)


def on_device(tokens, expert_ids, gates, w_gate, w_up, w_down, grad_out):
    token_count, model_width = tokens.shape
    chosen = expert_ids.shape[1]
    ep_size = lax.axis_size("ep")
    tp_size = lax.axis_size("tp")
    capacity = tp_size * max(
        1, min(token_count, 3 * token_count * chosen // (2 * ep_size)) // tp_size
    )
    me = lax.axis_index("ep")
    group = 8
    groups = ep_size // group
    all_tokens = ep_size * token_count
    routing = jnp.concatenate([expert_ids.astype(jnp.float32), gates], axis=1)
    both = jnp.concatenate([tokens, grad_out], axis=1)
    own_kernels = ep_size == 8 * Z and tp_size == 1
    if own_kernels:
        routing = jnp.pad(routing, ((0, 0), (0, 128 - 2 * chosen)))
        both_all, all_routing = gather(both, routing, ep_size)
    else:
        all_routing = lax.all_gather(routing, "ep", axis=0, tiled=True)
        both_all = lax.all_gather(both, "ep", axis=0, tiled=True)
    all_ids = all_routing[:, :chosen]
    all_gates = all_routing[:, chosen : 2 * chosen]
    hit = all_ids == me.astype(jnp.float32)
    token_gate = jnp.sum(jnp.where(hit, all_gates, 0.0), axis=1)
    token_hit = jnp.any(hit, axis=1).reshape(ep_size, token_count)
    counted = token_hit.astype(jnp.int32)
    slot = jnp.cumsum(counted, axis=1) - counted
    place = jnp.where(token_hit, slot, -1).reshape(groups, group, token_count)
    same = jnp.eye(group, dtype=jnp.bool_)[None, :, None, :, None]
    pick = (
        same
        & (
            place[:, None, None, :, :]
            == jnp.arange(capacity, dtype=jnp.int32)[None, None, :, None, None]
        )
    ).reshape(groups, group * capacity, group * token_count)
    picker = pick.astype(jnp.bfloat16)
    row_gate = jnp.sum(
        jnp.where(pick, token_gate.reshape(groups, 1, group * token_count), 0.0), axis=2
    ).reshape(-1, 1)
    rows = ep_size * capacity

    def take(full):
        return (
            lax.dot_general(
                picker,
                full.reshape(groups, group * token_count, 2 * model_width),
                (((2,), (1,)), ((0,), (0,))),
                preferred_element_type=jnp.float32,
            )
            .astype(jnp.bfloat16)
            .reshape(rows, 2 * model_width)
        )

    def put(part):
        return (
            lax.dot_general(
                picker,
                part.reshape(groups, group * capacity, -1),
                (((1,), (1,)), ((0,), (0,))),
                preferred_element_type=jnp.float32,
            )
            .astype(jnp.bfloat16)
            .reshape(all_tokens, -1)
        )

    gate_mat = w_gate[0]
    up_mat = w_up[0]
    down_mat = w_down[0]
    contract = (((1,), (1,)), ((), ()))
    over_rows = (((0,), (0,)), ((), ()))
    plain = (((1,), (0,)), ((), ()))
    f32 = jnp.float32
    both_rows = take(both_all)
    x_rows, d_rows = both_rows[:, :model_width], both_rows[:, model_width:]
    pre_gate = lax.dot_general(x_rows, gate_mat, contract, preferred_element_type=f32)
    pre_up = lax.dot_general(x_rows, up_mat, contract, preferred_element_type=f32)
    sig = jax.nn.sigmoid(pre_gate)
    activated = pre_gate * sig
    hidden = activated * pre_up
    hidden_gated = (hidden * row_gate).astype(jnp.bfloat16)
    out_rows = lax.dot_general(hidden_gated, down_mat, plain, preferred_element_type=f32)
    raw_hidden = lax.dot_general(d_rows, down_mat, contract, preferred_element_type=f32)
    row_dot = jnp.sum(raw_hidden * hidden, axis=1, keepdims=True)
    grad_hidden = raw_hidden * row_gate
    d_up = (grad_hidden * activated).astype(jnp.bfloat16)
    d_gate = (grad_hidden * pre_up * sig * (1.0 + pre_gate * (1.0 - sig))).astype(jnp.bfloat16)
    back_rows = lax.dot_general(d_gate, gate_mat, plain, preferred_element_type=f32)
    back_rows = back_rows + lax.dot_general(d_up, up_mat, plain, preferred_element_type=f32)
    row_choice = lax.dot_general(
        picker,
        hit.astype(jnp.bfloat16).reshape(groups, group * token_count, chosen),
        (((2,), (1,)), ((0,), (0,))),
        preferred_element_type=f32,
    ).reshape(rows, chosen)
    high = row_dot.astype(jnp.bfloat16)
    low = (row_dot - high.astype(f32)).astype(jnp.bfloat16)
    choice = row_choice.astype(jnp.bfloat16)
    extra = jnp.concatenate([high * choice, low * choice], axis=1)
    extra = jnp.pad(extra, ((0, 0), (0, 128 - 2 * chosen)))
    result_rows = jnp.concatenate(
        [out_rows.astype(jnp.bfloat16), back_rows.astype(jnp.bfloat16), extra], axis=1
    )
    partial = put(result_rows)
    if own_kernels:
        summed = scatter(partial, token_count)
    else:
        summed = lax.psum_scatter(partial, "ep", scatter_dimension=0, tiled=True)
    if tp_size > 1:
        summed = lax.psum(summed, "tp")
    dots = summed[:, 2 * model_width :].astype(f32)
    gate_grads = dots[:, :chosen] + dots[:, chosen : 2 * chosen]
    down_grad = lax.dot_general(hidden_gated, d_rows, over_rows, preferred_element_type=f32)
    gate_weight_grad = lax.dot_general(d_gate, x_rows, over_rows, preferred_element_type=f32)
    up_weight_grad = lax.dot_general(d_up, x_rows, over_rows, preferred_element_type=f32)
    return (
        summed[:, :model_width],
        gate_grads,
        summed[:, model_width : 2 * model_width],
        gate_weight_grad.astype(jnp.bfloat16)[None],
        up_weight_grad.astype(jnp.bfloat16)[None],
        down_grad.astype(jnp.bfloat16)[None],
    )


def solution(mesh):
    placed = (
        P("ep", None),
        P("ep", None),
        P("ep", None),
        P("ep", "tp", None),
        P("ep", "tp", None),
        P("ep", "tp", None),
        P("ep", None),
    )
    return jax.shard_map(
        on_device,
        mesh=mesh,
        in_specs=placed,
        out_specs=(
            P("ep", None),
            P("ep", None),
            P("ep", None),
            P("ep", "tp", None),
            P("ep", "tp", None),
            P("ep", "tp", None),
        ),
        check_vma=False,
    )
```
